256 devices in a mesh: chan: 64 (over y, x_hi, z), seg: 4 (over x_lo, core).
Axes of the slice: x: 4 (x_hi: 2, x_lo: 2; x = x_hi * 2 + x_lo), y: 4, z: 8, core: 2. Of those that a mesh axis runs over, the one named last changes fastest.
Arguments:
- spectra: bfloat16 [4, 256, 4096], P('seg', 'chan'), may hold values from -6 to 6
- band_gain: float32 [2048], replicated, may hold values from 0.1 to 1
Outputs:
- correlations: float32 [256, 201, 256], P(('chan', 'seg'))
The draws below stay inside these ranges and needn't reach their ends.
All inputs are finite; a program needn't handle non-finite values.
Results may differ from the reference program's by a relative error of at most 0.0003.
Values may be sent and summed in bfloat16 or wider, within the bound.
A program may use at most 64 MiB of HBM per device.

```python
import math
import jax
import jax.numpy as jnp
from jax import lax

CH_DEV = 4
F = 2048
MAXLAG = 100
CHANNELS = 256
SEGS = 4
LAGS = 201


def with_spikes(entries, key, source, target, shards_of, factor):
    owner, partner = [(jnp.arange(entries.shape[dim]) // (entries.shape[dim] // shards_of)).reshape([-1 if axis == dim else 1 for axis in range(entries.ndim)]) for dim in (source, target)]
    chosen = jax.random.permutation(key, shards_of)[partner]
    strong = (owner == chosen) | (owner == (partner + shards_of // 2) % shards_of)
    return jnp.where(strong, factor * entries, entries)


def block_levels(own_key, dims, split, least, high):
    loudness, own = 1.0, jax.random.fold_in(own_key, 6)
    for axis_at, parts in split:
        draws = jnp.exp(jax.random.uniform(jax.random.fold_in(own, axis_at), (parts,), jnp.float32, least / len(split), high / len(split)))
        loudness = loudness * jnp.repeat(draws, dims[axis_at] // parts).reshape([-1 if axis == axis_at else 1 for axis in range(len(dims))])
    return loudness


def gaussian_with(key, shape, spread, bound, cuts, heavy, held_as=jnp.bfloat16):
    values = spread * jax.random.normal(key, shape, jnp.float32)
    if cuts:
        values = values * block_levels(key, shape, cuts, -0.22, 0.18)
    return jnp.clip(with_spikes(values, jax.random.fold_in(key, 3), *heavy), -bound, bound).astype(held_as)


def setup_inputs(seed: int = 0) -> dict:
    key_of = jax.random.split(jax.random.key(seed), 3)
    return {
        "spectra": gaussian_with(key_of[0], (SEGS, CHANNELS, 2 * F), 1.0, 6.0, ((0, 4), (1, 64)), (0, 1, 4, 2.0)),
        "band_gain": jnp.clip(jnp.exp(jax.random.uniform(key_of[1], (F,), jnp.float32, math.log(0.1), math.log(1.0))), 0.1, 1.0),
    }


def make_table(band_gain):
    half = band_gain.shape[0]
    bins = jnp.arange(half, dtype=jnp.int32)[:, None]
    lag_steps = jnp.arange(2 * MAXLAG + 1, dtype=jnp.int32)[None, :] - MAXLAG
    phase_index = jnp.mod(bins * lag_steps, 2 * half)
    angles = 2.0 * math.pi / (2 * half) * phase_index.astype(jnp.float32)
    weights = band_gain[:, None] / math.sqrt(half)
    return jnp.concatenate([weights * jnp.cos(angles), -weights * jnp.sin(angles)], 0).astype(jnp.float32)

def cross_spectra(left_rows, right_rows):
    half = left_rows.shape[-1] // 2
    left_real = left_rows[..., :half].astype(jnp.float32)[..., :, None, :]
    left_imag = left_rows[..., half:].astype(jnp.float32)[..., :, None, :]
    right_real = right_rows[..., :half].astype(jnp.float32)[..., None, :, :]
    right_imag = right_rows[..., half:].astype(jnp.float32)[..., None, :, :]
    real_part = left_real * right_real + left_imag * right_imag
    imag_part = left_imag * right_real - left_real * right_imag
    return jnp.concatenate([real_part, imag_part], -1)

def reference(spectra, band_gain):
    lag_table = make_table(band_gain)
    blocks = spectra.reshape(SEGS, CHANNELS // CH_DEV, CH_DEV, 2 * F).transpose(1, 0, 2, 3)

    def rows_block(own_rows):
        products = cross_spectra(own_rows, spectra)
        return jnp.einsum('sijf,fl->ilj', products, lag_table, precision=lax.Precision.HIGHEST)
    result = lax.map(rows_block, blocks)
    return result.reshape(CHANNELS, LAGS, CHANNELS)
```

```python
import functools
import math

import jax
import jax.numpy as jnp
from jax import lax
from jax.experimental import pallas as pl
from jax.experimental.pallas import tpu as pltpu
from jax.sharding import PartitionSpec as P

MAXLAG = 100
MESH = pl.DeviceIdType.MESH


def place():
    c, s = lax.axis_index("chan"), lax.axis_index("seg")
    return (lax.rem(c // 8, 2) * 2 + s // 2, c // 16, lax.rem(c, 8), lax.rem(s, 2))


def device(x, y, z, core):
    return (y * 16 + (x // 2) * 8 + z, lax.rem(x, 2) * 2 + core)


def split(value):
    high = value.astype(jnp.bfloat16)
    return high, (value - high.astype(jnp.float32)).astype(jnp.bfloat16)


def kernel(x_ref, g_ref, out_ref, own, ibuf, jbuf, ifull, jfull, zh, zl, th, tl, base, steps,
           obuf, rbuf, own_sem, isend, irecv, jsend, jrecv, ksend, osend, orecv):
    x, y, z, k = place()
    xh, xl = x // 2, lax.rem(x, 2)
    half = g_ref.shape[1]
    tiles = half // 128

    barrier = pltpu.get_barrier_semaphore()
    load = pltpu.make_async_copy(x_ref.at[0], own, own_sem)
    load.start()

    def tell(target, me_too):
        @pl.when(jnp.logical_not(me_too))
        def _():
            pl.semaphore_signal(barrier, inc=1, device_id=target, device_id_type=MESH)

    @pl.loop(0, 16)
    def _(n):
        sy, ss = n // 4, lax.rem(n, 4)
        sx, sk = k * 2 + ss // 2, lax.rem(ss, 2)
        tell(device(sx, sy, z, sk), (sx == x) & (sy == y) & (sk == k))

    @pl.loop(0, 8)
    def _(n):
        sz, sx = (n // 2) * 2 + xl, xh * 2 + lax.rem(n, 2)
        tell(device(sx, y, sz, k), (sx == x) & (sz == z))

    tell(device(x, y, z, 1 - k), False)

    i_self = (k == xh).astype(jnp.int32)
    j_self = (lax.rem(z, 2) == xl).astype(jnp.int32)
    load.wait()
    pl.semaphore_wait(barrier, 25 - i_self - j_self)

    my_i_slot = y * 4 + xl * 2 + k
    my_j_slot = (z // 2) * 4 + xl * 2 + k

    def i_copy(n):
        tx, ty = lax.rem(x + n // 4, 4), lax.rem(y + n, 4)
        there = device(tx, ty, z, xh)
        return pltpu.make_async_remote_copy(own, ibuf.at[my_i_slot], isend.at[n], irecv.at[my_i_slot],
                                            device_id=there, device_id_type=MESH)

    def j_copy(n):
        tx, tz = xh * 2 + lax.rem(z, 2), lax.rem(z + n, 8)
        there = device(tx, y, tz, k)
        return pltpu.make_async_remote_copy(own, jbuf.at[my_j_slot], jsend.at[n], jrecv.at[my_j_slot],
                                            device_id=there, device_id_type=MESH)

    i_mine = pltpu.make_async_copy(own, ibuf.at[my_i_slot], irecv.at[my_i_slot])
    j_mine = pltpu.make_async_copy(own, jbuf.at[my_j_slot], jrecv.at[my_j_slot])

    @pl.loop(1, 8)
    def _(n):
        j_copy(n).start()

    @pl.loop(1, 16)
    def _(n):
        i_copy(n).start()

    @pl.when(j_self == 1)
    def _():
        j_mine.start()

    @pl.when(j_self == 0)
    def _():
        j_copy(0).start()

    @pl.when(i_self == 1)
    def _():
        i_mine.start()

    @pl.when(i_self == 0)
    def _():
        i_copy(0).start()

    def phases(first, step, rows):
        f = lax.broadcasted_iota(jnp.int32, (rows, 256), 0) * step + first
        lag = lax.broadcasted_iota(jnp.int32, (rows, 256), 1) - MAXLAG
        turn = jnp.bitwise_and(f * lag + half, 2 * half - 1) - half
        return turn.astype(jnp.float32) * (math.pi / half)

    angle = phases(0, 1, 128)
    base[0] = jnp.cos(angle)
    base[1] = jnp.sin(angle)
    angle = phases(0, 128, tiles)
    steps[0] = jnp.cos(angle)
    steps[1] = jnp.sin(angle)

    @pl.loop(0, tiles)
    def _(t):
        c, s = steps[0, pl.ds(t, 1), :], steps[1, pl.ds(t, 1), :]
        high, low = split(base[0] * c - base[1] * s)
        th[t, 0:128], tl[t, 0:128] = high, low
        high, low = split(base[1] * c + base[0] * s)
        th[t, 128:256], tl[t, 128:256] = high, low

    def relay(n):
        slot = n * 2 + k
        return pltpu.make_async_remote_copy(jbuf.at[slot], jbuf.at[slot], ksend.at[n], jrecv.at[slot],
                                            device_id=device(x, y, z, 1 - k), device_id_type=MESH)

    def landed(buf, sem, slot):
        pltpu.make_async_copy(buf.at[slot], buf.at[slot], sem.at[slot]).wait()

    @pl.loop(0, 8)
    def _(n):
        landed(jbuf, jrecv, n * 2 + k)
        relay(n).start()

    gain = g_ref[...] * (1.0 / math.sqrt(half))

    @pl.loop(0, 16)
    def _(n):
        landed(ibuf, irecv, n)
        ifull[n, :, 0:half] = ibuf[n, :, 0:half].astype(jnp.float32) * gain
        ifull[n, :, half:] = ibuf[n, :, half:].astype(jnp.float32) * gain

    @pl.loop(0, 8)
    def _(n):
        landed(jbuf, jrecv, n * 2 + 1 - k)

    @pl.loop(0, 4)
    def _(s):
        for p in range(2):
            jfull[s, p] = jnp.concatenate(
                [jbuf[8 * p + s].astype(jnp.float32), jbuf[8 * p + 4 + s].astype(jnp.float32)], 0)

    @pl.loop(0, tiles)
    def _(t):
        re = pl.ds(pl.multiple_of(t * 128, 128), 128)
        im = pl.ds(pl.multiple_of(half + t * 128, 128), 128)
        jr = [[jfull[s, p, :, re] for p in range(2)] for s in range(4)]
        ji = [[jfull[s, p, :, im] for p in range(2)] for s in range(4)]
        for i in range(16):
            ir = [ifull[(i // 4) * 4 + s, i % 4:i % 4 + 1, re] for s in range(4)]
            ii = [ifull[(i // 4) * 4 + s, i % 4:i % 4 + 1, im] for s in range(4)]
            zr, zi = [], []
            for p in range(2):
                zr.append(sum(ir[s] * jr[s][p] + ii[s] * ji[s][p] for s in range(4)))
                zi.append(sum(ir[s] * ji[s][p] - ii[s] * jr[s][p] for s in range(4)))
            high, low = split(jnp.concatenate(zr, 0))
            zh[t, i * 16:i * 16 + 16, 0:128], zl[t, i * 16:i * 16 + 16, 0:128] = high, low
            high, low = split(jnp.concatenate(zi, 0))
            zh[t, i * 16:i * 16 + 16, 128:256], zl[t, i * 16:i * 16 + 16, 128:256] = high, low

    obuf[...] = jnp.zeros_like(obuf)

    @pl.loop(0, tiles)
    def _(t):
        dot = functools.partial(jnp.dot, preferred_element_type=jnp.float32)
        obuf[...] += dot(zh[t], th[t]) + dot(zl[t], th[t]) + dot(zh[t], tl[t])

    my_o_slot = y * 4 + x

    def o_copy(i):
        there = device(k * 2 + lax.rem(i, 4) // 2, i // 4, z, lax.rem(i, 2))
        return pltpu.make_async_remote_copy(obuf.at[pl.ds(pl.multiple_of(i * 16, 16), 16)], rbuf.at[my_o_slot], osend.at[i],
                                            orecv.at[my_o_slot], device_id=there, device_id_type=MESH)

    own_row = my_i_slot

    @pl.loop(0, 16)
    def _(i):
        mine = (i_self == 1) & (i == own_row)

        @pl.when(mine)
        def _():
            pltpu.make_async_copy(obuf.at[pl.ds(pl.multiple_of(i * 16, 16), 16)], rbuf.at[my_o_slot], orecv.at[my_o_slot]).start()

        @pl.when(jnp.logical_not(mine))
        def _():
            o_copy(i).start()

    @pl.loop(0, 16)
    def _(n):
        landed(rbuf, orecv, n)

    for b in range(8):
        rows = []
        for m in range(4):
            rows += [rbuf[2 * b, 4 * m:4 * m + 4, :], rbuf[2 * b + 1, 4 * m:4 * m + 4, :]]
        joined = jnp.concatenate(rows, 0)
        base[b // 4, (b % 4) * 32:(b % 4) * 32 + 32, :] = joined

    for h in range(2):
        out_ref[0, :, h * 128:(h + 1) * 128] = base[h].T[0:2 * MAXLAG + 1]

    @pl.loop(1, 8)
    def _(n):
        j_copy(n).wait_send()

    @pl.loop(1, 16)
    def _(n):
        i_copy(n).wait_send()

    @pl.when(j_self == 0)
    def _():
        j_copy(0).wait_send()

    @pl.when(i_self == 0)
    def _():
        i_copy(0).wait_send()

    @pl.loop(0, 8)
    def _(n):
        relay(n).wait_send()

    @pl.loop(0, 16)
    def _(i):
        @pl.when(jnp.logical_not((i_self == 1) & (i == own_row)))
        def _():
            o_copy(i).wait_send()


def body(spectra, band_gain):
    half = band_gain.shape[0]
    tiles = half // 128
    f32, b16 = jnp.float32, jnp.bfloat16
    dma = pltpu.SemaphoreType.DMA
    return pl.pallas_call(
        kernel,
        out_shape=jax.ShapeDtypeStruct((1, 2 * MAXLAG + 1, 256), f32),
        in_specs=[pl.BlockSpec(memory_space=pl.ANY), pl.BlockSpec(memory_space=pltpu.VMEM)],
        out_specs=pl.BlockSpec(memory_space=pltpu.VMEM),
        scratch_shapes=[
            pltpu.VMEM((4, 2 * half), b16),
            pltpu.VMEM((16, 4, 2 * half), b16),
            pltpu.VMEM((16, 4, 2 * half), b16),
            pltpu.VMEM((16, 4, 2 * half), f32),
            pltpu.VMEM((4, 2, 8, 2 * half), f32),
            pltpu.VMEM((tiles, 256, 256), b16),
            pltpu.VMEM((tiles, 256, 256), b16),
            pltpu.VMEM((tiles, 256, 256), b16),
            pltpu.VMEM((tiles, 256, 256), b16),
            pltpu.VMEM((2, 128, 256), f32),
            pltpu.VMEM((2, tiles, 256), f32),
            pltpu.VMEM((256, 256), f32),
            pltpu.VMEM((16, 16, 256), f32),
            dma, dma((16,)), dma((16,)), dma((8,)), dma((16,)), dma((8,)), dma((16,)), dma((16,)),
        ],
        compiler_params=pltpu.CompilerParams(
            collective_id=0, has_side_effects=True, vmem_limit_bytes=48 * 2**20),
        name="correlate",
    )(spectra, band_gain.reshape(1, half))


def solution(mesh):
    return jax.shard_map(
        body,
        mesh=mesh,
        in_specs=(P("seg", "chan", None), P()),
        out_specs=P(("chan", "seg"), None, None),
        check_vma=False,
    )
```

```python
import functools
import math

import jax
import jax.numpy as jnp
from jax import lax
from jax.experimental import pallas as pl
from jax.experimental.pallas import tpu as pltpu
from jax.sharding import PartitionSpec as P

MAXLAG = 100
MESH = pl.DeviceIdType.MESH
BEHIND = [2, 3, 1, 0]
STAGED = False


def place():
    c, s = lax.axis_index("chan"), lax.axis_index("seg")
    return (lax.rem(c // 8, 2) * 2 + s // 2, c // 16, lax.rem(c, 8), lax.rem(s, 2))


def device(x, y, z, core):
    return (y * 16 + (x // 2) * 8 + z, lax.rem(x, 2) * 2 + core)


def split(value):
    high = value.astype(jnp.bfloat16)
    return high, (value - high.astype(jnp.float32)).astype(jnp.bfloat16)


def added(terms):
    return (terms[0] + terms[1]) + (terms[2] + terms[3])


def either(condition, yes, no):
    pl.when(condition)(yes)
    pl.when(jnp.logical_not(condition))(no)


def kernel(x_ref, g_ref, out_ref, own, gains, ibuf, jbuf, ifull, jfull, zh, zl, th, tl, base, steps,
           obuf, rbuf, own_sem, gain_sem, isend, irecv, jsend, jrecv, ksend, krecv, osend, orecv):
    x, y, z, k = place()
    xh, xl = x // 2, lax.rem(x, 2)
    half = x_ref.shape[2] // 2
    tiles = half // 128
    group = z // 4

    barrier = pltpu.get_barrier_semaphore()

    def signal(target):
        pl.semaphore_signal(barrier, inc=1, device_id=target, device_id_type=MESH)

    load = pltpu.make_async_copy(x_ref.at[0], own, own_sem)
    load.start()
    load_gain = pltpu.make_async_copy(g_ref, gains, gain_sem)
    load_gain.start()

    @pl.loop(0, 8)
    def _(n):
        sx, sz = xh * 2 + lax.rem(n, 2), (n // 2) * 2 + xl
        pl.when(jnp.logical_not((sx == x) & (sz == z)))(lambda: signal(device(sx, y, sz, k)))

    @pl.loop(0, 16)
    def _(n):
        sy, ss = n // 4, lax.rem(n, 4)
        sx, sk = k * 2 + ss // 2, lax.rem(ss, 2)
        pl.when(jnp.logical_not((sx == x) & (sy == y) & (sk == k)))(lambda: signal(device(sx, sy, z, sk)))

    signal(device(x, y, z, 1 - k))

    def phases(first, step, rows):
        f = lax.broadcasted_iota(jnp.int32, (rows, 256), 0) * step + first
        lag = lax.broadcasted_iota(jnp.int32, (rows, 256), 1) - MAXLAG
        turn = jnp.bitwise_and(f * lag + half, 2 * half - 1) - half
        return turn.astype(jnp.float32) * (math.pi / half)

    angle = phases(0, 1, 128)
    base[0] = jnp.cos(angle)
    base[1] = jnp.sin(angle)
    angle = phases(0, 128, tiles)
    steps[0] = jnp.cos(angle)
    steps[1] = jnp.sin(angle)

    i_self = k == xh
    j_self = lax.rem(z, 2) == xl
    load.wait()
    load_gain.wait()
    pl.semaphore_wait(barrier, 25 - i_self.astype(jnp.int32) - j_self.astype(jnp.int32))

    my_seg = xl * 2 + k
    my_j = lax.rem(z // 2, 2) * 2 + xl

    def ring_sends(g):
        @pl.loop(0, 4)
        def _(n):
            tz = g * 4 + lax.rem(z + 2 + n, 4)
            either(j_self & (tz == z),
                   lambda: pltpu.make_async_copy(own, jbuf.at[k, group, my_j], jrecv.at[group]).start(),
                   lambda: pltpu.make_async_remote_copy(
                       own, jbuf.at[k, group, my_j], jsend.at[g], jrecv.at[group],
                       device_id=device(xh * 2 + lax.rem(z, 2), y, tz, k), device_id_type=MESH).start())

    def plane_send(dx, dy):
        spot = BEHIND.index((4 - dy) % 4)
        pltpu.make_async_remote_copy(own, ibuf.at[spot * 4 + my_seg], isend, irecv.at[spot // 2],
                                     device_id=device(lax.rem(x + dx, 4), lax.rem(y + dy, 4), z, xh), device_id_type=MESH).start()

    def left(ref, sem):
        return lambda: pltpu.make_async_copy(ref, ref, sem).wait()

    def ring_left(g):
        either(j_self & (group == g), left(ibuf.at[pl.ds(0, 3)], jsend.at[g]), left(ibuf.at[pl.ds(0, 4)], jsend.at[g]))

    ring_sends(0)
    for spot in range(4):
        dy = (4 - BEHIND[spot]) % 4
        for dx in (2, 1, 3):
            plane_send(dx, dy)
        if dy:
            plane_send(0, dy)
        else:
            either(i_self, lambda: pltpu.make_async_copy(own, ibuf.at[12 + my_seg], irecv.at[1]).start(), lambda: plane_send(0, 0))
    if not STAGED:
        ring_sends(1)

    @pl.loop(0, tiles)
    def _(t):
        c, s = steps[0, pl.ds(t, 1), :], steps[1, pl.ds(t, 1), :]
        th[t, 0:128], tl[t, 0:128] = split(base[0] * c - base[1] * s)
        th[t, 128:256], tl[t, 128:256] = split(base[1] * c + base[0] * s)

    if STAGED:
        ring_left(0)
        ring_sends(1)

    def here(buf, sem):
        pltpu.make_async_copy(buf, buf, sem).wait()

    for turn in range(2):
        g = group if turn == 0 else 1 - group
        here(jbuf.at[k, g], jrecv.at[g])
        pltpu.make_async_remote_copy(jbuf.at[k, g], jbuf.at[k, g], ksend.at[g], krecv.at[g],
                                     device_id=device(x, y, z, 1 - k), device_id_type=MESH).start()

    dot = functools.partial(jnp.dot, preferred_element_type=jnp.float32)
    scale = 1.0 / math.sqrt(half)
    my_o = y * 4 + x

    for part in range(2):
        here(ibuf.at[pl.ds(8 * part, 8)], irecv.at[part])

        @pl.loop(0, 2)
        def _(n, part=part):
            for s in range(4):
                real = ibuf[8 * part + 4 * n + s, :, 0:half].astype(jnp.float32) * (gains[...] * scale)
                imag = ibuf[8 * part + 4 * n + s, :, half:].astype(jnp.float32) * (gains[...] * scale)
                ifull[n, s, :, 0:half] = real
                ifull[n, s, :, half:2 * half] = imag
                ifull[n, s, :, 2 * half:] = real + imag

        if part == 0:
            for g in range(2):
                here(jbuf.at[1 - k, g], krecv.at[g])
            for s in range(4):
                for g in range(2):
                    jfull[s, g] = jnp.concatenate([jbuf[s % 2, g, s // 2].astype(jnp.float32),
                                                   jbuf[s % 2, g, 2 + s // 2].astype(jnp.float32)], 0)

        @pl.loop(0, tiles)
        def _(t):
            re = pl.ds(pl.multiple_of(t * 128, 128), 128)
            im = pl.ds(pl.multiple_of(half + t * 128, 128), 128)
            both = pl.ds(pl.multiple_of(2 * half + t * 128, 128), 128)
            jr = [[jfull[s, g, :, re] for g in range(2)] for s in range(4)]
            ji = [[jfull[s, g, :, im] for g in range(2)] for s in range(4)]
            jd = [[jr[s][g] - ji[s][g] for g in range(2)] for s in range(4)]
            for i in range(8):
                ib = [ifull[i // 4, s, i % 4:i % 4 + 1, both] for s in range(4)]
                ir = [ifull[i // 4, s, i % 4:i % 4 + 1, re] for s in range(4)]
                ii = [ifull[i // 4, s, i % 4:i % 4 + 1, im] for s in range(4)]
                zr, zi = [], []
                for g in range(2):
                    rr = added([ir[s] * jr[s][g] for s in range(4)])
                    ss = added([ii[s] * ji[s][g] for s in range(4)])
                    bd = added([ib[s] * jd[s][g] for s in range(4)])
                    zr.append(rr + ss)
                    zi.append((rr - ss) - bd)
                rows = slice(i * 16, i * 16 + 16)
                zh[t, rows, 0:128], zl[t, rows, 0:128] = split(jnp.concatenate(zr, 0))
                zh[t, rows, 128:256], zl[t, rows, 128:256] = split(jnp.concatenate(zi, 0))

        total = None
        for t in range(tiles):
            term = dot(zh[t], th[t]) + dot(zl[t], th[t]) + dot(zh[t], tl[t])
            total = term if total is None else total + term
        obuf[part] = total

        for n in range(8):
            spot, r = 2 * part + n // 4, n % 4
            block = obuf.at[part, pl.ds(n * 16, 16)]

            def give(block=block, spot=spot, r=r):
                pltpu.make_async_remote_copy(
                    block, rbuf.at[my_o], osend, orecv,
                    device_id=device(k * 2 + r // 2, lax.rem(y + BEHIND[spot], 4), z, r % 2), device_id_type=MESH).start()

            if BEHIND[spot]:
                give()
            else:
                either(i_self & (my_seg == r), lambda block=block: pltpu.make_async_copy(block, rbuf.at[my_o], orecv).start(), give)

    either(i_self, left(rbuf.at[pl.ds(0, 15)], osend), left(rbuf, osend))
    either(i_self, left(ibuf.at[pl.ds(0, 15)], isend), left(ibuf, isend))

    for g in range(1 if STAGED else 0, 2):
        ring_left(g)
    for g in range(2):
        pltpu.make_async_copy(jbuf.at[0, g], jbuf.at[0, g], ksend.at[g]).wait()

    here(rbuf, orecv)
    for b in range(8):
        rows = []
        for m in range(4):
            rows += [rbuf[2 * b, 4 * m:4 * m + 4, :], rbuf[2 * b + 1, 4 * m:4 * m + 4, :]]
        base[b // 4, (b % 4) * 32:(b % 4) * 32 + 32, :] = jnp.concatenate(rows, 0)

    for h in range(2):
        out_ref[0, :, h * 128:(h + 1) * 128] = base[h].T[0:2 * MAXLAG + 1]


def body(spectra, band_gain):
    half = band_gain.shape[0]
    tiles = half // 128
    f32, b16 = jnp.float32, jnp.bfloat16
    dma = pltpu.SemaphoreType.DMA
    return pl.pallas_call(
        kernel,
        out_shape=jax.ShapeDtypeStruct((1, 2 * MAXLAG + 1, 256), f32),
        in_specs=[pl.BlockSpec(memory_space=pltpu.HBM), pl.BlockSpec(memory_space=pltpu.HBM)],
        out_specs=pl.BlockSpec(memory_space=pltpu.VMEM),
        scratch_shapes=[
            pltpu.VMEM((4, 2 * half), b16),
            pltpu.VMEM((1, half), f32),
            pltpu.VMEM((16, 4, 2 * half), b16),
            pltpu.VMEM((2, 2, 4, 4, 2 * half), b16),
            pltpu.VMEM((2, 4, 4, 3 * half), f32),
            pltpu.VMEM((4, 2, 8, 2 * half), f32),
            pltpu.VMEM((tiles, 128, 256), b16),
            pltpu.VMEM((tiles, 128, 256), b16),
            pltpu.VMEM((tiles, 256, 256), b16),
            pltpu.VMEM((tiles, 256, 256), b16),
            pltpu.VMEM((2, 128, 256), f32),
            pltpu.VMEM((2, tiles, 256), f32),
            pltpu.VMEM((2, 128, 256), f32),
            pltpu.VMEM((16, 16, 256), f32),
            dma, dma, dma, dma((2,)), dma((2,)), dma((2,)), dma((2,)), dma((2,)), dma, dma,
        ],
        compiler_params=pltpu.CompilerParams(
            collective_id=0, has_side_effects=True, vmem_limit_bytes=48 * 2**20),
        name="correlate",
    )(spectra, band_gain.reshape(1, half))


def solution(mesh):
    return jax.shard_map(
        body,
        mesh=mesh,
        in_specs=(P("seg", "chan", None), P()),
        out_specs=P(("chan", "seg"), None, None),
        check_vma=False,
    )
```

```python
import functools
import math

import jax
import jax.numpy as jnp
from jax import lax
from jax.experimental import pallas as pl
from jax.experimental.pallas import tpu as pltpu
from jax.sharding import PartitionSpec as P

MAXLAG = 100
MESH = pl.DeviceIdType.MESH
BEHIND = [2, 3, 1, 0]
STAGED = False


def place():
    c, s = lax.axis_index("chan"), lax.axis_index("seg")
    return (lax.rem(c // 8, 2) * 2 + s // 2, c // 16, lax.rem(c, 8), lax.rem(s, 2))


def device(x, y, z, core):
    return (y * 16 + (x // 2) * 8 + z, lax.rem(x, 2) * 2 + core)


def split(value):
    high = value.astype(jnp.bfloat16)
    return high, (value - high.astype(jnp.float32)).astype(jnp.bfloat16)


def added(terms):
    return (terms[0] + terms[1]) + (terms[2] + terms[3])


def either(condition, yes, no):
    pl.when(condition)(yes)
    pl.when(jnp.logical_not(condition))(no)


def kernel(x_ref, g_ref, rbuf, own, gains, ibuf, jbuf, ifull, jfull, zh, zl, th, tl, base, steps,
           obuf, own_sem, gain_sem, isend, irecv, jsend, jrecv, ksend, krecv, osend, orecv):
    x, y, z, k = place()
    xh, xl = x // 2, lax.rem(x, 2)
    half = x_ref.shape[2] // 2
    tiles = half // 128
    group = z // 4

    barrier = pltpu.get_barrier_semaphore()

    def signal(target):
        pl.semaphore_signal(barrier, inc=1, device_id=target, device_id_type=MESH)

    load = pltpu.make_async_copy(x_ref.at[0], own, own_sem)
    load.start()
    load_gain = pltpu.make_async_copy(g_ref, gains, gain_sem)
    load_gain.start()

    @pl.loop(0, 8)
    def _(n):
        sx, sz = xh * 2 + lax.rem(n, 2), (n // 2) * 2 + xl
        pl.when(jnp.logical_not((sx == x) & (sz == z)))(lambda: signal(device(sx, y, sz, k)))

    @pl.loop(0, 16)
    def _(n):
        sy, ss = n // 4, lax.rem(n, 4)
        sx, sk = k * 2 + ss // 2, lax.rem(ss, 2)
        pl.when(jnp.logical_not((sx == x) & (sy == y) & (sk == k)))(lambda: signal(device(sx, sy, z, sk)))

    signal(device(x, y, z, 1 - k))

    def phases(first, step, rows):
        f = lax.broadcasted_iota(jnp.int32, (rows, 256), 0) * step + first
        lag = lax.broadcasted_iota(jnp.int32, (rows, 256), 1) - MAXLAG
        turn = jnp.bitwise_and(f * lag + half, 2 * half - 1) - half
        return turn.astype(jnp.float32) * (math.pi / half)

    angle = phases(0, 1, 128)
    base[0] = jnp.cos(angle)
    base[1] = jnp.sin(angle)
    angle = phases(0, 128, tiles)
    steps[0] = jnp.cos(angle)
    steps[1] = jnp.sin(angle)

    i_self = k == xh
    j_self = lax.rem(z, 2) == xl
    load.wait()
    load_gain.wait()
    pl.semaphore_wait(barrier, 25 - i_self.astype(jnp.int32) - j_self.astype(jnp.int32))

    my_seg = xl * 2 + k
    my_j = lax.rem(z // 2, 2) * 2 + xl

    def ring_sends(g):
        @pl.loop(0, 4)
        def _(n):
            tz = g * 4 + lax.rem(z + 2 + n, 4)
            either(j_self & (tz == z),
                   lambda: pltpu.make_async_copy(own, jbuf.at[k, group, my_j], jrecv.at[group]).start(),
                   lambda: pltpu.make_async_remote_copy(
                       own, jbuf.at[k, group, my_j], jsend.at[g], jrecv.at[group],
                       device_id=device(xh * 2 + lax.rem(z, 2), y, tz, k), device_id_type=MESH).start())

    def plane_send(dx, dy):
        spot = BEHIND.index((4 - dy) % 4)
        pltpu.make_async_remote_copy(own, ibuf.at[spot * 4 + my_seg], isend, irecv.at[spot // 2],
                                     device_id=device(lax.rem(x + dx, 4), lax.rem(y + dy, 4), z, xh), device_id_type=MESH).start()

    def left(ref, sem):
        return lambda: pltpu.make_async_copy(ref, ref, sem).wait()

    def ring_left(g):
        either(j_self & (group == g), left(ibuf.at[pl.ds(0, 3)], jsend.at[g]), left(ibuf.at[pl.ds(0, 4)], jsend.at[g]))

    ring_sends(0)
    for spot in range(4):
        dy = (4 - BEHIND[spot]) % 4
        for dx in (2, 1, 3):
            plane_send(dx, dy)
        if dy:
            plane_send(0, dy)
        else:
            either(i_self, lambda: pltpu.make_async_copy(own, ibuf.at[12 + my_seg], irecv.at[1]).start(), lambda: plane_send(0, 0))
    if not STAGED:
        ring_sends(1)

    @pl.loop(0, tiles)
    def _(t):
        c, s = steps[0, pl.ds(t, 1), :], steps[1, pl.ds(t, 1), :]
        th[t, 0:128], tl[t, 0:128] = split(base[0] * c - base[1] * s)
        th[t, 128:256], tl[t, 128:256] = split(base[1] * c + base[0] * s)

    if STAGED:
        ring_left(0)
        ring_sends(1)

    def here(buf, sem):
        pltpu.make_async_copy(buf, buf, sem).wait()

    for turn in range(2):
        g = group if turn == 0 else 1 - group
        here(jbuf.at[k, g], jrecv.at[g])
        pltpu.make_async_remote_copy(jbuf.at[k, g], jbuf.at[k, g], ksend.at[g], krecv.at[g],
                                     device_id=device(x, y, z, 1 - k), device_id_type=MESH).start()

    dot = functools.partial(jnp.dot, preferred_element_type=jnp.float32)
    scale = 1.0 / math.sqrt(half)
    my_o = y * 4 + x

    for part in range(2):
        here(ibuf.at[pl.ds(8 * part, 8)], irecv.at[part])

        @pl.loop(0, 2)
        def _(n, part=part):
            for s in range(4):
                real = ibuf[8 * part + 4 * n + s, :, 0:half].astype(jnp.float32) * (gains[...] * scale)
                imag = ibuf[8 * part + 4 * n + s, :, half:].astype(jnp.float32) * (gains[...] * scale)
                ifull[n, s, :, 0:half] = real
                ifull[n, s, :, half:2 * half] = imag
                ifull[n, s, :, 2 * half:] = real + imag

        if part == 0:
            for g in range(2):
                here(jbuf.at[1 - k, g], krecv.at[g])
            for s in range(4):
                for g in range(2):
                    jfull[s, g] = jnp.concatenate([jbuf[s % 2, g, s // 2].astype(jnp.float32),
                                                   jbuf[s % 2, g, 2 + s // 2].astype(jnp.float32)], 0)

        @pl.loop(0, tiles)
        def _(t):
            re = pl.ds(pl.multiple_of(t * 128, 128), 128)
            im = pl.ds(pl.multiple_of(half + t * 128, 128), 128)
            both = pl.ds(pl.multiple_of(2 * half + t * 128, 128), 128)
            jr = [[jfull[s, g, :, re] for g in range(2)] for s in range(4)]
            ji = [[jfull[s, g, :, im] for g in range(2)] for s in range(4)]
            jd = [[jr[s][g] - ji[s][g] for g in range(2)] for s in range(4)]
            for i in range(8):
                ib = [ifull[i // 4, s, i % 4:i % 4 + 1, both] for s in range(4)]
                ir = [ifull[i // 4, s, i % 4:i % 4 + 1, re] for s in range(4)]
                ii = [ifull[i // 4, s, i % 4:i % 4 + 1, im] for s in range(4)]
                zr, zi = [], []
                for g in range(2):
                    rr = added([ir[s] * jr[s][g] for s in range(4)])
                    ss = added([ii[s] * ji[s][g] for s in range(4)])
                    bd = added([ib[s] * jd[s][g] for s in range(4)])
                    zr.append(rr + ss)
                    zi.append((rr - ss) - bd)
                rows = slice(i * 16, i * 16 + 16)
                zh[t, rows, 0:128], zl[t, rows, 0:128] = split(jnp.concatenate(zr, 0))
                zh[t, rows, 128:256], zl[t, rows, 128:256] = split(jnp.concatenate(zi, 0))

        total = None
        for t in range(tiles):
            term = dot(zh[t], th[t]) + dot(zl[t], th[t]) + dot(zh[t], tl[t])
            total = term if total is None else total + term
        obuf[part] = total

        for n in range(8):
            spot, r = 2 * part + n // 4, n % 4
            block = obuf.at[part, pl.ds(n * 16, 16)]

            def give(block=block, spot=spot, r=r):
                pltpu.make_async_remote_copy(
                    block, rbuf.at[my_o], osend, orecv,
                    device_id=device(k * 2 + r // 2, lax.rem(y + BEHIND[spot], 4), z, r % 2), device_id_type=MESH).start()

            if BEHIND[spot]:
                give()
            else:
                either(i_self & (my_seg == r), lambda block=block: pltpu.make_async_copy(block, rbuf.at[my_o], orecv).start(), give)

    either(i_self, left(rbuf.at[pl.ds(0, 15)], osend), left(rbuf, osend))
    either(i_self, left(ibuf.at[pl.ds(0, 15)], isend), left(ibuf, isend))

    for g in range(1 if STAGED else 0, 2):
        ring_left(g)
    for g in range(2):
        pltpu.make_async_copy(jbuf.at[0, g], jbuf.at[0, g], ksend.at[g]).wait()

    here(rbuf, orecv)


def assemble(rbuf, out_ref, base):
    for b in range(8):
        rows = []
        for m in range(4):
            rows += [rbuf[2 * b, 4 * m:4 * m + 4, :], rbuf[2 * b + 1, 4 * m:4 * m + 4, :]]
        base[b // 4, (b % 4) * 32:(b % 4) * 32 + 32, :] = jnp.concatenate(rows, 0)

    for h in range(2):
        out_ref[:, 0, h * 128:(h + 1) * 128] = base[h].T[0:2 * MAXLAG + 1]


def body(spectra, band_gain):
    half = band_gain.shape[0]
    tiles = half // 128
    f32, b16 = jnp.float32, jnp.bfloat16
    dma = pltpu.SemaphoreType.DMA
    blocks = pl.pallas_call(
        kernel,
        out_shape=jax.ShapeDtypeStruct((16, 16, 256), f32),
        in_specs=[pl.BlockSpec(memory_space=pltpu.HBM), pl.BlockSpec(memory_space=pltpu.HBM)],
        out_specs=pl.BlockSpec(memory_space=pl.ANY),
        scratch_shapes=[
            pltpu.VMEM((4, 2 * half), b16),
            pltpu.VMEM((1, half), f32),
            pltpu.VMEM((16, 4, 2 * half), b16),
            pltpu.VMEM((2, 2, 4, 4, 2 * half), b16),
            pltpu.VMEM((2, 4, 4, 3 * half), f32),
            pltpu.VMEM((4, 2, 8, 2 * half), f32),
            pltpu.VMEM((tiles, 128, 256), b16),
            pltpu.VMEM((tiles, 128, 256), b16),
            pltpu.VMEM((tiles, 256, 256), b16),
            pltpu.VMEM((tiles, 256, 256), b16),
            pltpu.VMEM((2, 128, 256), f32),
            pltpu.VMEM((2, tiles, 256), f32),
            pltpu.VMEM((2, 128, 256), f32),
            dma, dma, dma, dma((2,)), dma((2,)), dma((2,)), dma((2,)), dma((2,)), dma, dma,
        ],
        compiler_params=pltpu.CompilerParams(
            collective_id=0, has_side_effects=True, vmem_limit_bytes=58 * 2**20),
        name="correlate",
    )(spectra, band_gain.reshape(1, half))
    rows = pl.pallas_call(
        assemble,
        out_shape=jax.ShapeDtypeStruct((2 * MAXLAG + 1, 1, 256), f32),
        in_specs=[pl.BlockSpec(memory_space=pltpu.VMEM)],
        out_specs=pl.BlockSpec(memory_space=pltpu.VMEM),
        scratch_shapes=[pltpu.VMEM((2, 128, 256), f32)],
        name="assemble",
    )(blocks)
    return jnp.transpose(rows, (1, 0, 2))


def solution(mesh):
    return jax.shard_map(
        body,
        mesh=mesh,
        in_specs=(P("seg", "chan", None), P()),
        out_specs=P(("chan", "seg"), None, None),
        check_vma=False,
    )
```

```python
import functools
import math

import jax
import jax.numpy as jnp
from jax import lax
from jax.experimental import pallas as pl
from jax.experimental.pallas import tpu as pltpu
from jax.sharding import PartitionSpec as P

MAXLAG = 100
MESH = pl.DeviceIdType.MESH
BEHIND = [2, 3, 1, 0]
STAGED = False
ROWS = 8


def place():
    c, s = lax.axis_index("chan"), lax.axis_index("seg")
    return (lax.rem(c // 8, 2) * 2 + s // 2, c // 16, lax.rem(c, 8), lax.rem(s, 2))


def device(x, y, z, core):
    return (y * 16 + (x // 2) * 8 + z, lax.rem(x, 2) * 2 + core)


def split(value):
    high = value.astype(jnp.bfloat16)
    return high, (value - high.astype(jnp.float32)).astype(jnp.bfloat16)


def added(terms):
    return (terms[0] + terms[1]) + (terms[2] + terms[3])


def either(condition, yes, no):
    pl.when(condition)(yes)
    pl.when(jnp.logical_not(condition))(no)


def kernel(x_ref, g_ref, rbuf, own, gains, ibuf, jbuf, ifull, jfull, zh, zl, wh, wl, steps,
           obuf, own_sem, gain_sem, isend, irecv, jsend, jrecv, ksend, krecv, osend, orecv):
    x, y, z, k = place()
    xh, xl = x // 2, lax.rem(x, 2)
    half = x_ref.shape[2] // 2
    group = z // 4

    barrier = pltpu.get_barrier_semaphore()

    def signal(target):
        pl.semaphore_signal(barrier, inc=1, device_id=target, device_id_type=MESH)

    load = pltpu.make_async_copy(x_ref.at[0], own, own_sem)
    load.start()
    load_gain = pltpu.make_async_copy(g_ref, gains, gain_sem)
    load_gain.start()

    @pl.loop(0, 8)
    def _(n):
        sx, sz = xh * 2 + lax.rem(n, 2), (n // 2) * 2 + xl
        pl.when(jnp.logical_not((sx == x) & (sz == z)))(lambda: signal(device(sx, y, sz, k)))

    @pl.loop(0, 16)
    def _(n):
        sy, ss = n // 4, lax.rem(n, 4)
        sx, sk = k * 2 + ss // 2, lax.rem(ss, 2)
        pl.when(jnp.logical_not((sx == x) & (sy == y) & (sk == k)))(lambda: signal(device(sx, sy, z, sk)))

    signal(device(x, y, z, 1 - k))

    def phases(step, rows):
        f = lax.broadcasted_iota(jnp.int32, (rows, 128), 0) * step
        lag = lax.broadcasted_iota(jnp.int32, (rows, 128), 1)
        turn = jnp.bitwise_and(f * lag + half, 2 * half - 1) - half
        return turn.astype(jnp.float32) * (math.pi / half)

    angle = phases(1, 256)
    wh[:, 0:128], wl[:, 0:128] = split(jnp.cos(angle))
    wh[:, 128:256], wl[:, 128:256] = split(jnp.sin(angle))
    angle = phases(256, half // 256)
    steps[0] = jnp.cos(angle)
    steps[1] = jnp.sin(angle)

    i_self = k == xh
    j_self = lax.rem(z, 2) == xl
    load.wait()
    load_gain.wait()
    pl.semaphore_wait(barrier, 25 - i_self.astype(jnp.int32) - j_self.astype(jnp.int32))

    my_seg = xl * 2 + k
    my_j = lax.rem(z // 2, 2) * 2 + xl

    def ring_sends(g):
        @pl.loop(0, 4)
        def _(n):
            tz = g * 4 + lax.rem(z + 2 + n, 4)
            either(j_self & (tz == z),
                   lambda: pltpu.make_async_copy(own, jbuf.at[k, group, my_j], jrecv.at[group]).start(),
                   lambda: pltpu.make_async_remote_copy(
                       own, jbuf.at[k, group, my_j], jsend.at[g], jrecv.at[group],
                       device_id=device(xh * 2 + lax.rem(z, 2), y, tz, k), device_id_type=MESH).start())

    def plane_send(dx, dy):
        spot = BEHIND.index((4 - dy) % 4)
        pltpu.make_async_remote_copy(own, ibuf.at[spot * 4 + my_seg], isend, irecv.at[spot // 2],
                                     device_id=device(lax.rem(x + dx, 4), lax.rem(y + dy, 4), z, xh), device_id_type=MESH).start()

    def left(ref, sem):
        return lambda: pltpu.make_async_copy(ref, ref, sem).wait()

    def ring_left(g):
        either(j_self & (group == g), left(ibuf.at[pl.ds(0, 3)], jsend.at[g]), left(ibuf.at[pl.ds(0, 4)], jsend.at[g]))

    ring_sends(0)
    for spot in range(4):
        dy = (4 - BEHIND[spot]) % 4
        for dx in (2, 1, 3):
            plane_send(dx, dy)
        if dy:
            plane_send(0, dy)
        else:
            either(i_self, lambda: pltpu.make_async_copy(own, ibuf.at[12 + my_seg], irecv.at[1]).start(), lambda: plane_send(0, 0))
    if not STAGED:
        ring_sends(1)

    if STAGED:
        ring_left(0)
        ring_sends(1)

    def here(buf, sem):
        pltpu.make_async_copy(buf, buf, sem).wait()

    for turn in range(2):
        g = group if turn == 0 else 1 - group
        here(jbuf.at[k, g], jrecv.at[g])
        pltpu.make_async_remote_copy(jbuf.at[k, g], jbuf.at[k, g], ksend.at[g], krecv.at[g],
                                     device_id=device(x, y, z, 1 - k), device_id_type=MESH).start()

    dot = functools.partial(jnp.dot, preferred_element_type=jnp.float32)
    scale = 1.0 / math.sqrt(half)
    my_o = y * 4 + x

    for part in range(16 // ROWS):
        if part * ROWS % 8 == 0:
            here(ibuf.at[pl.ds(part * ROWS, 8)], irecv.at[part * ROWS // 8])

        @pl.loop(0, ROWS // 4)
        def _(n, part=part):
            for s in range(4):
                real = ibuf[ROWS * part + 4 * n + s, :, 0:half].astype(jnp.float32) * (gains[...] * scale)
                imag = ibuf[ROWS * part + 4 * n + s, :, half:].astype(jnp.float32) * (gains[...] * scale)
                ifull[n, s, :, 0:half] = real
                ifull[n, s, :, half:2 * half] = imag
                ifull[n, s, :, 2 * half:] = real + imag

        if part == 0:
            for g in range(2):
                here(jbuf.at[1 - k, g], krecv.at[g])
            for s in range(4):
                for g in range(2):
                    jfull[s, g] = jnp.concatenate([jbuf[s % 2, g, s // 2].astype(jnp.float32),
                                                   jbuf[s % 2, g, 2 + s // 2].astype(jnp.float32)], 0)

        def cross(t, u):
            offset = t * 256 + u * 128
            re = pl.ds(pl.multiple_of(offset, 128), 128)
            im = pl.ds(pl.multiple_of(half + offset, 128), 128)
            both = pl.ds(pl.multiple_of(2 * half + offset, 128), 128)
            cut = slice(u * 128, u * 128 + 128)
            jr = [[jfull[s, g, :, re] for g in range(2)] for s in range(4)]
            ji = [[jfull[s, g, :, im] for g in range(2)] for s in range(4)]
            jd = [[jr[s][g] - ji[s][g] for g in range(2)] for s in range(4)]
            for i in range(ROWS):
                ib = [ifull[i // 4, s, i % 4:i % 4 + 1, both] for s in range(4)]
                ir = [ifull[i // 4, s, i % 4:i % 4 + 1, re] for s in range(4)]
                ii = [ifull[i // 4, s, i % 4:i % 4 + 1, im] for s in range(4)]
                zr, zi = [], []
                for g in range(2):
                    rr = added([ir[s] * jr[s][g] for s in range(4)])
                    ss = added([ii[s] * ji[s][g] for s in range(4)])
                    bd = added([ib[s] * jd[s][g] for s in range(4)])
                    zr.append(rr + ss)
                    zi.append((rr - ss) - bd)
                for value, first in ((zr, 0), (zi, 16 * ROWS)):
                    rows = slice(first + i * 16, first + i * 16 + 16)
                    zh[t, rows, cut], zl[t, rows, cut] = split(jnp.concatenate(value, 0))

        @pl.loop(0, half // 256)
        def _(t, cross=cross):
            for u in range(2):
                cross(t, u)

        even = odd = 0.0
        edge = 16 * ROWS
        for t in range(half // 256):
            near = dot(zh[t], wh[...]) + dot(zl[t], wh[...]) + dot(zh[t], wl[...])
            c, d = steps[0, t:t + 1, :], steps[1, t:t + 1, :]
            even += c * near[0:edge, 0:128] - d * near[0:edge, 128:256]
            odd += d * near[edge:, 0:128] + c * near[edge:, 128:256]
        obuf[part, :, 0:128] = even + odd
        obuf[part, :, 128:256] = even - odd

        for n in range(ROWS):
            spot, r = part * ROWS // 4 + n // 4, n % 4
            block = obuf.at[part, pl.ds(n * 16, 16)]

            def give(block=block, spot=spot, r=r):
                pltpu.make_async_remote_copy(
                    block, rbuf.at[my_o], osend, orecv,
                    device_id=device(k * 2 + r // 2, lax.rem(y + BEHIND[spot], 4), z, r % 2), device_id_type=MESH).start()

            if BEHIND[spot]:
                give()
            else:
                either(i_self & (my_seg == r), lambda block=block: pltpu.make_async_copy(block, rbuf.at[my_o], orecv).start(), give)

    either(i_self, left(rbuf.at[pl.ds(0, 15)], osend), left(rbuf, osend))
    either(i_self, left(ibuf.at[pl.ds(0, 15)], isend), left(ibuf, isend))

    for g in range(1 if STAGED else 0, 2):
        ring_left(g)
    for g in range(2):
        pltpu.make_async_copy(jbuf.at[0, g], jbuf.at[0, g], ksend.at[g]).wait()

    here(rbuf, orecv)


def assemble(rbuf, out_ref, base, turned):
    for b in range(8):
        rows = []
        for m in range(4):
            rows += [rbuf[2 * b, 4 * m:4 * m + 4, :], rbuf[2 * b + 1, 4 * m:4 * m + 4, :]]
        base[b // 4, (b % 4) * 32:(b % 4) * 32 + 32, :] = jnp.concatenate(rows, 0)

    for h in range(2):
        cut = slice(h * 128, (h + 1) * 128)
        turned[...] = base[h].T
        out_ref[MAXLAG:, 0, cut] = turned[0:MAXLAG + 1]
        for lag in range(1, MAXLAG + 1):
            out_ref[MAXLAG - lag:MAXLAG - lag + 1, 0, cut] = turned[128 + lag:129 + lag]


def body(spectra, band_gain):
    half = band_gain.shape[0]
    f32, b16 = jnp.float32, jnp.bfloat16
    dma = pltpu.SemaphoreType.DMA
    blocks = pl.pallas_call(
        kernel,
        out_shape=jax.ShapeDtypeStruct((16, 16, 256), f32),
        in_specs=[pl.BlockSpec(memory_space=pltpu.HBM), pl.BlockSpec(memory_space=pltpu.HBM)],
        out_specs=pl.BlockSpec(memory_space=pl.ANY),
        scratch_shapes=[
            pltpu.VMEM((4, 2 * half), b16),
            pltpu.VMEM((1, half), f32),
            pltpu.VMEM((16, 4, 2 * half), b16),
            pltpu.VMEM((2, 2, 4, 4, 2 * half), b16),
            pltpu.VMEM((2, 4, 4, 3 * half), f32),
            pltpu.VMEM((4, 2, 8, 2 * half), f32),
            pltpu.VMEM((half // 256, 32 * ROWS, 256), b16),
            pltpu.VMEM((half // 256, 32 * ROWS, 256), b16),
            pltpu.VMEM((256, 256), b16),
            pltpu.VMEM((256, 256), b16),
            pltpu.VMEM((2, half // 256, 128), f32),
            pltpu.VMEM((16 // ROWS, 16 * ROWS, 256), f32),
            dma, dma, dma, dma((2,)), dma((2,)), dma((2,)), dma((2,)), dma((2,)), dma, dma,
        ],
        compiler_params=pltpu.CompilerParams(
            collective_id=0, has_side_effects=True, vmem_limit_bytes=58 * 2**20),
        name="correlate",
    )(spectra, band_gain.reshape(1, half))
    rows = pl.pallas_call(
        assemble,
        out_shape=jax.ShapeDtypeStruct((2 * MAXLAG + 1, 1, 256), f32),
        in_specs=[pl.BlockSpec(memory_space=pltpu.VMEM)],
        out_specs=pl.BlockSpec(memory_space=pltpu.VMEM),
        scratch_shapes=[pltpu.VMEM((2, 128, 256), f32), pltpu.VMEM((256, 128), f32)],
        name="assemble",
    )(blocks)
    return jnp.transpose(rows, (1, 0, 2))


def solution(mesh):
    return jax.shard_map(
        body,
        mesh=mesh,
        in_specs=(P("seg", "chan", None), P()),
        out_specs=P(("chan", "seg"), None, None),
        check_vma=False,
    )
```

```python
import functools
import math

import jax
import jax.numpy as jnp
from jax import lax
from jax.experimental import pallas as pl
from jax.experimental.pallas import tpu as pltpu
from jax.sharding import PartitionSpec as P

MAXLAG = 100
MESH = pl.DeviceIdType.MESH
BEHIND = [2, 3, 1, 0]
STAGED = False
ROWS = 8


def place():
    c, s = lax.axis_index("chan"), lax.axis_index("seg")
    return (lax.rem(c // 8, 2) * 2 + s // 2, c // 16, lax.rem(c, 8), lax.rem(s, 2))


def device(x, y, z, core):
    return (y * 16 + (x // 2) * 8 + z, lax.rem(x, 2) * 2 + core)


def split(value):
    high = value.astype(jnp.bfloat16)
    return high, (value - high.astype(jnp.float32)).astype(jnp.bfloat16)


def added(terms):
    return sum(terms[1:], terms[0]) if len(terms) < 4 else (terms[0] + terms[1]) + (terms[2] + terms[3])


def either(condition, yes, no):
    pl.when(condition)(yes)
    pl.when(jnp.logical_not(condition))(no)


def kernel(x_ref, g_ref, rbuf, own, gains, ibuf, jbuf, ifull, jfull, zfirst, zh, zl, wh, wl, steps,
           obuf, own_sem, gain_sem, isend, irecv, jsend, jrecv, ksend, krecv, osend, orecv):
    x, y, z, k = place()
    xh, xl = x // 2, lax.rem(x, 2)
    half = x_ref.shape[2] // 2
    group = z // 4

    barrier = pltpu.get_barrier_semaphore()

    def signal(target):
        pl.semaphore_signal(barrier, inc=1, device_id=target, device_id_type=MESH)

    load = pltpu.make_async_copy(x_ref.at[0], own, own_sem)
    load.start()
    load_gain = pltpu.make_async_copy(g_ref, gains, gain_sem)
    load_gain.start()

    @pl.loop(0, 8)
    def _(n):
        sx, sz = xh * 2 + lax.rem(n, 2), (n // 2) * 2 + xl
        pl.when(jnp.logical_not((sx == x) & (sz == z)))(lambda: signal(device(sx, y, sz, k)))

    @pl.loop(0, 16)
    def _(n):
        sy, ss = n // 4, lax.rem(n, 4)
        sx, sk = k * 2 + ss // 2, lax.rem(ss, 2)
        pl.when(jnp.logical_not((sx == x) & (sy == y) & (sk == k)))(lambda: signal(device(sx, sy, z, sk)))

    signal(device(x, y, z, 1 - k))

    def phases(step, rows):
        f = lax.broadcasted_iota(jnp.int32, (rows, 128), 0) * step
        lag = lax.broadcasted_iota(jnp.int32, (rows, 128), 1)
        turn = jnp.bitwise_and(f * lag + half, 2 * half - 1) - half
        return turn.astype(jnp.float32) * (math.pi / half)

    angle = phases(1, 256)
    wh[:, 0:128], wl[:, 0:128] = split(jnp.cos(angle))
    wh[:, 128:256], wl[:, 128:256] = split(jnp.sin(angle))
    angle = phases(256, half // 256)
    steps[0] = jnp.cos(angle)
    steps[1] = jnp.sin(angle)

    i_self = k == xh
    j_self = lax.rem(z, 2) == xl
    load.wait()
    load_gain.wait()
    pl.semaphore_wait(barrier, 25 - i_self.astype(jnp.int32) - j_self.astype(jnp.int32))

    my_seg = xl * 2 + k
    my_j = lax.rem(z // 2, 2) * 2 + xl

    def ring_sends(g):
        @pl.loop(0, 4)
        def _(n):
            tz = g * 4 + n
            either(j_self & (tz == z),
                   lambda: pltpu.make_async_copy(own, jbuf.at[k, group, my_j], jrecv.at[group * 4 + my_j]).start(),
                   lambda: pltpu.make_async_remote_copy(
                       own, jbuf.at[k, group, my_j], jsend.at[g], jrecv.at[group * 4 + my_j],
                       device_id=device(xh * 2 + lax.rem(z, 2), y, tz, k), device_id_type=MESH).start())

    def plane_send(dx, dy):
        spot = BEHIND.index((4 - dy) % 4)
        pltpu.make_async_remote_copy(own, ibuf.at[spot * 4 + my_seg], isend, irecv.at[spot // 2],
                                     device_id=device(lax.rem(x + dx, 4), lax.rem(y + dy, 4), z, xh), device_id_type=MESH).start()

    def left(ref, sem):
        return lambda: pltpu.make_async_copy(ref, ref, sem).wait()

    def ring_left(g):
        either(j_self & (group == g), left(ibuf.at[pl.ds(0, 3)], jsend.at[g]), left(ibuf.at[pl.ds(0, 4)], jsend.at[g]))

    ring_sends(0)
    for spot in range(4):
        dy = (4 - BEHIND[spot]) % 4
        for dx in (2, 1, 3):
            plane_send(dx, dy)
        if dy:
            plane_send(0, dy)
        else:
            either(i_self, lambda: pltpu.make_async_copy(own, ibuf.at[12 + my_seg], irecv.at[1]).start(), lambda: plane_send(0, 0))
    if not STAGED:
        ring_sends(1)

    if STAGED:
        ring_left(0)
        ring_sends(1)

    def here(buf, sem):
        pltpu.make_async_copy(buf, buf, sem).wait()

    for turn in range(2):
        g = group if turn == 0 else 1 - group
        for n in range(4):
            here(jbuf.at[k, g, n], jrecv.at[g * 4 + n])
            pltpu.make_async_remote_copy(jbuf.at[k, g, n], jbuf.at[k, g, n], ksend, krecv.at[g],
                                         device_id=device(x, y, z, 1 - k), device_id_type=MESH).start()

    dot = functools.partial(jnp.dot, preferred_element_type=jnp.float32)
    scale = 1.0 / math.sqrt(half)
    my_o = y * 4 + x

    for part in range(16 // ROWS):
        if part * ROWS % 8 == 0:
            here(ibuf.at[pl.ds(part * ROWS, 8)], irecv.at[part * ROWS // 8])

        @pl.loop(0, ROWS // 4)
        def _(n, part=part):
            for s in range(4):
                real = ibuf[ROWS * part + 4 * n + s, :, 0:half].astype(jnp.float32) * (gains[...] * scale)
                imag = ibuf[ROWS * part + 4 * n + s, :, half:].astype(jnp.float32) * (gains[...] * scale)
                ifull[n, s, :, 0:half] = real
                ifull[n, s, :, half:2 * half] = imag
                ifull[n, s, :, 2 * half:] = real + imag

        def cross(t, u, segments, turn):
            offset = t * 256 + u * 128
            re = pl.ds(pl.multiple_of(offset, 128), 128)
            im = pl.ds(pl.multiple_of(half + offset, 128), 128)
            both = pl.ds(pl.multiple_of(2 * half + offset, 128), 128)
            cut = slice(u * 128, u * 128 + 128)
            jr = [[jfull[s, g, :, re] for g in range(2)] for s in segments]
            ji = [[jfull[s, g, :, im] for g in range(2)] for s in segments]
            jd = [[p[g] - q[g] for g in range(2)] for p, q in zip(jr, ji)]
            for i in range(ROWS):
                ib = [ifull[i // 4, s, i % 4:i % 4 + 1, both] for s in segments]
                ir = [ifull[i // 4, s, i % 4:i % 4 + 1, re] for s in segments]
                ii = [ifull[i // 4, s, i % 4:i % 4 + 1, im] for s in segments]
                zr, zi = [], []
                for g in range(2):
                    rr = added([p * q[g] for p, q in zip(ir, jr)])
                    ss = added([p * q[g] for p, q in zip(ii, ji)])
                    bd = added([p * q[g] for p, q in zip(ib, jd)])
                    zr.append(rr + ss)
                    zi.append((rr - ss) - bd)
                for value, first in ((zr, 0), (zi, 16 * ROWS)):
                    rows = slice(first + i * 16, first + i * 16 + 16)
                    value = jnp.concatenate(value, 0)
                    if turn == 0:
                        zfirst[t, rows, cut] = value
                    else:
                        zh[t, rows, cut], zl[t, rows, cut] = split(zfirst[t, rows, cut] + value if turn == 1 else value)

        for turn in ((0, 1) if part == 0 else (2,)):
            core = k if turn == 0 else 1 - k
            if turn == 1:
                for g in range(2):
                    here(jbuf.at[1 - k, g], krecv.at[g])
            if turn < 2:
                for a in range(2):
                    for g in range(2):
                        jfull[2 * a + core, g] = jnp.concatenate([jbuf[core, g, a].astype(jnp.float32),
                                                                  jbuf[core, g, 2 + a].astype(jnp.float32)], 0)
            segments = (core, 2 + core) if turn < 2 else (0, 1, 2, 3)

            @pl.loop(0, half // 256)
            def _(t, cross=cross, segments=segments, turn=turn):
                for u in range(2):
                    cross(t, u, segments, turn)

        even = odd = 0.0
        edge = 16 * ROWS
        for t in range(half // 256):
            near = dot(zh[t], wh[...]) + dot(zl[t], wh[...]) + dot(zh[t], wl[...])
            c, d = steps[0, t:t + 1, :], steps[1, t:t + 1, :]
            even += c * near[0:edge, 0:128] - d * near[0:edge, 128:256]
            odd += d * near[edge:, 0:128] + c * near[edge:, 128:256]
        obuf[part, :, 0:128] = even + odd
        obuf[part, :, 128:256] = even - odd

        for n in range(ROWS):
            spot, r = part * ROWS // 4 + n // 4, n % 4
            block = obuf.at[part, pl.ds(n * 16, 16)]

            def give(block=block, spot=spot, r=r):
                pltpu.make_async_remote_copy(
                    block, rbuf.at[my_o], osend, orecv,
                    device_id=device(k * 2 + r // 2, lax.rem(y + BEHIND[spot], 4), z, r % 2), device_id_type=MESH).start()

            if BEHIND[spot]:
                give()
            else:
                either(i_self & (my_seg == r), lambda block=block: pltpu.make_async_copy(block, rbuf.at[my_o], orecv).start(), give)

    either(i_self, left(rbuf.at[pl.ds(0, 15)], osend), left(rbuf, osend))
    either(i_self, left(ibuf.at[pl.ds(0, 15)], isend), left(ibuf, isend))

    for g in range(1 if STAGED else 0, 2):
        ring_left(g)
    here(jbuf.at[0], ksend)

    here(rbuf, orecv)


def assemble(rbuf, out_ref, base, turned):
    for b in range(8):
        rows = []
        for m in range(4):
            rows += [rbuf[2 * b, 4 * m:4 * m + 4, :], rbuf[2 * b + 1, 4 * m:4 * m + 4, :]]
        base[b // 4, (b % 4) * 32:(b % 4) * 32 + 32, :] = jnp.concatenate(rows, 0)

    for h in range(2):
        cut = slice(h * 128, (h + 1) * 128)
        turned[...] = base[h].T
        out_ref[MAXLAG:, 0, cut] = turned[0:MAXLAG + 1]
        for lag in range(1, MAXLAG + 1):
            out_ref[MAXLAG - lag:MAXLAG - lag + 1, 0, cut] = turned[128 + lag:129 + lag]


def body(spectra, band_gain):
    half = band_gain.shape[0]
    f32, b16 = jnp.float32, jnp.bfloat16
    dma = pltpu.SemaphoreType.DMA
    blocks = pl.pallas_call(
        kernel,
        out_shape=jax.ShapeDtypeStruct((16, 16, 256), f32),
        in_specs=[pl.BlockSpec(memory_space=pltpu.HBM), pl.BlockSpec(memory_space=pltpu.HBM)],
        out_specs=pl.BlockSpec(memory_space=pl.ANY),
        scratch_shapes=[
            pltpu.VMEM((4, 2 * half), b16),
            pltpu.VMEM((1, half), f32),
            pltpu.VMEM((16, 4, 2 * half), b16),
            pltpu.VMEM((2, 2, 4, 4, 2 * half), b16),
            pltpu.VMEM((2, 4, 4, 3 * half), f32),
            pltpu.VMEM((4, 2, 8, 2 * half), f32),
            pltpu.VMEM((half // 256, 32 * ROWS, 256), f32),
            pltpu.VMEM((half // 256, 32 * ROWS, 256), b16),
            pltpu.VMEM((half // 256, 32 * ROWS, 256), b16),
            pltpu.VMEM((256, 256), b16),
            pltpu.VMEM((256, 256), b16),
            pltpu.VMEM((2, half // 256, 128), f32),
            pltpu.VMEM((16 // ROWS, 16 * ROWS, 256), f32),
            dma, dma, dma, dma((2,)), dma((2,)), dma((8,)), dma, dma((2,)), dma, dma,
        ],
        compiler_params=pltpu.CompilerParams(
            collective_id=0, has_side_effects=True, vmem_limit_bytes=58 * 2**20),
        name="correlate",
    )(spectra, band_gain.reshape(1, half))
    rows = pl.pallas_call(
        assemble,
        out_shape=jax.ShapeDtypeStruct((2 * MAXLAG + 1, 1, 256), f32),
        in_specs=[pl.BlockSpec(memory_space=pltpu.VMEM)],
        out_specs=pl.BlockSpec(memory_space=pltpu.VMEM),
        scratch_shapes=[pltpu.VMEM((2, 128, 256), f32), pltpu.VMEM((256, 128), f32)],
        name="assemble",
    )(blocks)
    return jnp.transpose(rows, (1, 0, 2))


def solution(mesh):
    return jax.shard_map(
        body,
        mesh=mesh,
        in_specs=(P("seg", "chan", None), P()),
        out_specs=P(("chan", "seg"), None, None),
        check_vma=False,
    )
```

```python
import functools
import math

import jax
import jax.numpy as jnp
from jax import lax
from jax.experimental import pallas as pl
from jax.experimental.pallas import tpu as pltpu
from jax.sharding import PartitionSpec as P

MAXLAG = 100
MESH = pl.DeviceIdType.MESH
BEHIND = [2, 3, 1, 0]
STAGED = False
ROWS = 4


def place():
    c, s = lax.axis_index("chan"), lax.axis_index("seg")
    return (lax.rem(c // 8, 2) * 2 + s // 2, c // 16, lax.rem(c, 8), lax.rem(s, 2))


def device(x, y, z, core):
    return (y * 16 + (x // 2) * 8 + z, lax.rem(x, 2) * 2 + core)


def split(value):
    high = value.astype(jnp.bfloat16)
    return high, (value - high.astype(jnp.float32)).astype(jnp.bfloat16)


def added(terms):
    return (terms[0] + terms[1]) + (terms[2] + terms[3])


def either(condition, yes, no):
    pl.when(condition)(yes)
    pl.when(jnp.logical_not(condition))(no)


def kernel(x_ref, g_ref, rbuf, own, gains, ibuf, jbuf, ifull, jfull, zh, zl, wh, wl, steps,
           obuf, own_sem, gain_sem, isend, irecv, jsend, jrecv, ksend, krecv, osend, orecv):
    x, y, z, k = place()
    xh, xl = x // 2, lax.rem(x, 2)
    half = x_ref.shape[2] // 2
    group = z // 4

    barrier = pltpu.get_barrier_semaphore()

    def signal(target):
        pl.semaphore_signal(barrier, inc=1, device_id=target, device_id_type=MESH)

    load = pltpu.make_async_copy(x_ref.at[0], own, own_sem)
    load.start()
    load_gain = pltpu.make_async_copy(g_ref, gains, gain_sem)
    load_gain.start()

    @pl.loop(0, 8)
    def _(n):
        sx, sz = xh * 2 + lax.rem(n, 2), (n // 2) * 2 + xl
        pl.when(jnp.logical_not((sx == x) & (sz == z)))(lambda: signal(device(sx, y, sz, k)))

    @pl.loop(0, 16)
    def _(n):
        sy, ss = n // 4, lax.rem(n, 4)
        sx, sk = k * 2 + ss // 2, lax.rem(ss, 2)
        pl.when(jnp.logical_not((sx == x) & (sy == y) & (sk == k)))(lambda: signal(device(sx, sy, z, sk)))

    signal(device(x, y, z, 1 - k))

    def phases(step, rows):
        f = lax.broadcasted_iota(jnp.int32, (rows, 128), 0) * step
        lag = lax.broadcasted_iota(jnp.int32, (rows, 128), 1)
        turn = jnp.bitwise_and(f * lag + half, 2 * half - 1) - half
        return turn.astype(jnp.float32) * (math.pi / half)

    angle = phases(1, 256)
    wh[:, 0:128], wl[:, 0:128] = split(jnp.cos(angle))
    wh[:, 128:256], wl[:, 128:256] = split(jnp.sin(angle))
    angle = phases(256, half // 256)
    steps[0] = jnp.cos(angle)
    steps[1] = jnp.sin(angle)

    i_self = k == xh
    j_self = lax.rem(z, 2) == xl
    load.wait()
    load_gain.wait()
    pl.semaphore_wait(barrier, 25 - i_self.astype(jnp.int32) - j_self.astype(jnp.int32))

    my_seg = xl * 2 + k
    my_j = lax.rem(z // 2, 2) * 2 + xl

    def ring_sends(g):
        @pl.loop(0, 4)
        def _(n):
            tz = g * 4 + lax.rem(z + 2 + n, 4)
            either(j_self & (tz == z),
                   lambda: pltpu.make_async_copy(own, jbuf.at[k, group, my_j], jrecv.at[group]).start(),
                   lambda: pltpu.make_async_remote_copy(
                       own, jbuf.at[k, group, my_j], jsend.at[g], jrecv.at[group],
                       device_id=device(xh * 2 + lax.rem(z, 2), y, tz, k), device_id_type=MESH).start())

    def plane_send(dx, dy):
        spot = BEHIND.index((4 - dy) % 4)
        pltpu.make_async_remote_copy(own, ibuf.at[spot * 4 + my_seg], isend, irecv.at[spot],
                                     device_id=device(lax.rem(x + dx, 4), lax.rem(y + dy, 4), z, xh), device_id_type=MESH).start()

    def left(ref, sem):
        return lambda: pltpu.make_async_copy(ref, ref, sem).wait()

    def ring_left(g):
        either(j_self & (group == g), left(ibuf.at[pl.ds(0, 3)], jsend.at[g]), left(ibuf.at[pl.ds(0, 4)], jsend.at[g]))

    ring_sends(0)
    for spot in range(4):
        dy = (4 - BEHIND[spot]) % 4
        for dx in (2, 1, 3):
            plane_send(dx, dy)
        if dy:
            plane_send(0, dy)
        else:
            either(i_self, lambda: pltpu.make_async_copy(own, ibuf.at[12 + my_seg], irecv.at[3]).start(), lambda: plane_send(0, 0))
    if not STAGED:
        ring_sends(1)

    if STAGED:
        ring_left(0)
        ring_sends(1)

    def here(buf, sem):
        pltpu.make_async_copy(buf, buf, sem).wait()

    for turn in range(2):
        g = group if turn == 0 else 1 - group
        here(jbuf.at[k, g], jrecv.at[g])
        pltpu.make_async_remote_copy(jbuf.at[k, g], jbuf.at[k, g], ksend.at[g], krecv.at[g],
                                     device_id=device(x, y, z, 1 - k), device_id_type=MESH).start()

    dot = functools.partial(jnp.dot, preferred_element_type=jnp.float32)
    scale = 1.0 / math.sqrt(half)
    my_o = y * 4 + x

    for part in range(16 // ROWS):
        here(ibuf.at[pl.ds(part * ROWS, ROWS)], irecv.at[part])

        @pl.loop(0, ROWS // 4)
        def _(n, part=part):
            for s in range(4):
                real = ibuf[ROWS * part + 4 * n + s, :, 0:half].astype(jnp.float32) * (gains[...] * scale)
                imag = ibuf[ROWS * part + 4 * n + s, :, half:].astype(jnp.float32) * (gains[...] * scale)
                ifull[n, s, :, 0:half] = real
                ifull[n, s, :, half:2 * half] = imag
                ifull[n, s, :, 2 * half:] = real + imag

        if part == 0:
            for g in range(2):
                here(jbuf.at[1 - k, g], krecv.at[g])
            for s in range(4):
                for g in range(2):
                    jfull[s, g] = jnp.concatenate([jbuf[s % 2, g, s // 2].astype(jnp.float32),
                                                   jbuf[s % 2, g, 2 + s // 2].astype(jnp.float32)], 0)

        def cross(t, u):
            offset = t * 256 + u * 128
            re = pl.ds(pl.multiple_of(offset, 128), 128)
            im = pl.ds(pl.multiple_of(half + offset, 128), 128)
            both = pl.ds(pl.multiple_of(2 * half + offset, 128), 128)
            cut = slice(u * 128, u * 128 + 128)
            jr = [[jfull[s, g, :, re] for g in range(2)] for s in range(4)]
            ji = [[jfull[s, g, :, im] for g in range(2)] for s in range(4)]
            jd = [[jr[s][g] - ji[s][g] for g in range(2)] for s in range(4)]
            for i in range(ROWS):
                ib = [ifull[i // 4, s, i % 4:i % 4 + 1, both] for s in range(4)]
                ir = [ifull[i // 4, s, i % 4:i % 4 + 1, re] for s in range(4)]
                ii = [ifull[i // 4, s, i % 4:i % 4 + 1, im] for s in range(4)]
                zr, zi = [], []
                for g in range(2):
                    rr = added([ir[s] * jr[s][g] for s in range(4)])
                    ss = added([ii[s] * ji[s][g] for s in range(4)])
                    bd = added([ib[s] * jd[s][g] for s in range(4)])
                    zr.append(rr + ss)
                    zi.append((rr - ss) - bd)
                for value, first in ((zr, 0), (zi, 16 * ROWS)):
                    rows = slice(first + i * 16, first + i * 16 + 16)
                    zh[t, rows, cut], zl[t, rows, cut] = split(jnp.concatenate(value, 0))

        @pl.loop(0, half // 256)
        def _(t, cross=cross):
            for u in range(2):
                cross(t, u)

        even = odd = 0.0
        edge = 16 * ROWS
        for t in range(half // 256):
            near = dot(zh[t], wh[...]) + dot(zl[t], wh[...]) + dot(zh[t], wl[...])
            c, d = steps[0, t:t + 1, :], steps[1, t:t + 1, :]
            even += c * near[0:edge, 0:128] - d * near[0:edge, 128:256]
            odd += d * near[edge:, 0:128] + c * near[edge:, 128:256]
        obuf[part, :, 0:128] = even + odd
        obuf[part, :, 128:256] = even - odd

        for n in range(ROWS):
            spot, r = part * ROWS // 4 + n // 4, n % 4
            block = obuf.at[part, pl.ds(n * 16, 16)]

            def give(block=block, spot=spot, r=r):
                pltpu.make_async_remote_copy(
                    block, rbuf.at[my_o], osend, orecv,
                    device_id=device(k * 2 + r // 2, lax.rem(y + BEHIND[spot], 4), z, r % 2), device_id_type=MESH).start()

            if BEHIND[spot]:
                give()
            else:
                either(i_self & (my_seg == r), lambda block=block: pltpu.make_async_copy(block, rbuf.at[my_o], orecv).start(), give)

    either(i_self, left(rbuf.at[pl.ds(0, 15)], osend), left(rbuf, osend))
    either(i_self, left(ibuf.at[pl.ds(0, 15)], isend), left(ibuf, isend))

    for g in range(1 if STAGED else 0, 2):
        ring_left(g)
    for g in range(2):
        pltpu.make_async_copy(jbuf.at[0, g], jbuf.at[0, g], ksend.at[g]).wait()

    here(rbuf, orecv)


def assemble(rbuf, out_ref, base, turned):
    for b in range(8):
        rows = []
        for m in range(4):
            rows += [rbuf[2 * b, 4 * m:4 * m + 4, :], rbuf[2 * b + 1, 4 * m:4 * m + 4, :]]
        base[b // 4, (b % 4) * 32:(b % 4) * 32 + 32, :] = jnp.concatenate(rows, 0)

    for h in range(2):
        cut = slice(h * 128, (h + 1) * 128)
        turned[...] = base[h].T
        out_ref[MAXLAG:, 0, cut] = turned[0:MAXLAG + 1]
        for lag in range(1, MAXLAG + 1):
            out_ref[MAXLAG - lag:MAXLAG - lag + 1, 0, cut] = turned[128 + lag:129 + lag]


def body(spectra, band_gain):
    half = band_gain.shape[0]
    f32, b16 = jnp.float32, jnp.bfloat16
    dma = pltpu.SemaphoreType.DMA
    blocks = pl.pallas_call(
        kernel,
        out_shape=jax.ShapeDtypeStruct((16, 16, 256), f32),
        in_specs=[pl.BlockSpec(memory_space=pltpu.HBM), pl.BlockSpec(memory_space=pltpu.HBM)],
        out_specs=pl.BlockSpec(memory_space=pl.ANY),
        scratch_shapes=[
            pltpu.VMEM((4, 2 * half), b16),
            pltpu.VMEM((1, half), f32),
            pltpu.VMEM((16, 4, 2 * half), b16),
            pltpu.VMEM((2, 2, 4, 4, 2 * half), b16),
            pltpu.VMEM((2, 4, 4, 3 * half), f32),
            pltpu.VMEM((4, 2, 8, 2 * half), f32),
            pltpu.VMEM((half // 256, 32 * ROWS, 256), b16),
            pltpu.VMEM((half // 256, 32 * ROWS, 256), b16),
            pltpu.VMEM((256, 256), b16),
            pltpu.VMEM((256, 256), b16),
            pltpu.VMEM((2, half // 256, 128), f32),
            pltpu.VMEM((16 // ROWS, 16 * ROWS, 256), f32),
            dma, dma, dma, dma((4,)), dma((2,)), dma((2,)), dma((2,)), dma((2,)), dma, dma,
        ],
        compiler_params=pltpu.CompilerParams(
            collective_id=0, has_side_effects=True, vmem_limit_bytes=58 * 2**20),
        name="correlate",
    )(spectra, band_gain.reshape(1, half))
    rows = pl.pallas_call(
        assemble,
        out_shape=jax.ShapeDtypeStruct((2 * MAXLAG + 1, 1, 256), f32),
        in_specs=[pl.BlockSpec(memory_space=pltpu.VMEM)],
        out_specs=pl.BlockSpec(memory_space=pltpu.VMEM),
        scratch_shapes=[pltpu.VMEM((2, 128, 256), f32), pltpu.VMEM((256, 128), f32)],
        name="assemble",
    )(blocks)
    return jnp.transpose(rows, (1, 0, 2))


def solution(mesh):
    return jax.shard_map(
        body,
        mesh=mesh,
        in_specs=(P("seg", "chan", None), P()),
        out_specs=P(("chan", "seg"), None, None),
        check_vma=False,
    )
```

```python
import functools
import math

import jax
import jax.numpy as jnp
from jax import lax
from jax.experimental import pallas as pl
from jax.experimental.pallas import tpu as pltpu
from jax.sharding import PartitionSpec as P

MAXLAG = 100
MESH = pl.DeviceIdType.MESH
BEHIND = [2, 3, 1, 0]
STAGED = False
ROWS = 4


def place():
    c, s = lax.axis_index("chan"), lax.axis_index("seg")
    return (lax.rem(c // 8, 2) * 2 + s // 2, c // 16, lax.rem(c, 8), lax.rem(s, 2))


def device(x, y, z, core):
    return (y * 16 + (x // 2) * 8 + z, lax.rem(x, 2) * 2 + core)


def split(value):
    high = value.astype(jnp.bfloat16)
    return high, (value - high.astype(jnp.float32)).astype(jnp.bfloat16)


def added(terms):
    return (terms[0] + terms[1]) + (terms[2] + terms[3])


def either(condition, yes, no):
    pl.when(condition)(yes)
    pl.when(jnp.logical_not(condition))(no)


def kernel(x_ref, g_ref, rbuf, own, gains, ibuf, jbuf, ifull, jfull, zh, zl, wh, wl, steps,
           obuf, own_sem, gain_sem, isend, irecv, jsend, jrecv, ksend, krecv, osend, orecv):
    x, y, z, k = place()
    xh, xl = x // 2, lax.rem(x, 2)
    half = x_ref.shape[2] // 2
    group = z // 4

    barrier = pltpu.get_barrier_semaphore()

    def signal(target):
        pl.semaphore_signal(barrier, inc=1, device_id=target, device_id_type=MESH)

    load = pltpu.make_async_copy(x_ref.at[0], own, own_sem)
    load.start()
    load_gain = pltpu.make_async_copy(g_ref, gains, gain_sem)
    load_gain.start()

    @pl.loop(0, 8)
    def _(n):
        sx, sz = xh * 2 + lax.rem(n, 2), (n // 2) * 2 + xl
        pl.when(jnp.logical_not((sx == x) & (sz == z)))(lambda: signal(device(sx, y, sz, k)))

    @pl.loop(0, 16)
    def _(n):
        sy, ss = n // 4, lax.rem(n, 4)
        sx, sk = k * 2 + ss // 2, lax.rem(ss, 2)
        pl.when(jnp.logical_not((sx == x) & (sy == y) & (sk == k)))(lambda: signal(device(sx, sy, z, sk)))

    signal(device(x, y, z, 1 - k))

    def phases(step, rows):
        f = lax.broadcasted_iota(jnp.int32, (rows, 128), 0) * step
        lag = lax.broadcasted_iota(jnp.int32, (rows, 128), 1)
        turn = jnp.bitwise_and(f * lag + half, 2 * half - 1) - half
        return turn.astype(jnp.float32) * (math.pi / half)

    angle = phases(1, 256)
    wh[:, 0:128], wl[:, 0:128] = split(jnp.cos(angle))
    wh[:, 128:256], wl[:, 128:256] = split(jnp.sin(angle))
    angle = phases(256, half // 256)
    steps[0] = jnp.cos(angle)
    steps[1] = jnp.sin(angle)

    i_self = k == xh
    j_self = lax.rem(z, 2) == xl
    load.wait()
    load_gain.wait()
    pl.semaphore_wait(barrier, 25 - i_self.astype(jnp.int32) - j_self.astype(jnp.int32))

    my_seg = xl * 2 + k
    my_j = lax.rem(z // 2, 2) * 2 + xl

    def ring_sends(g):
        @pl.loop(0, 4)
        def _(n):
            tz = g * 4 + n
            either(j_self & (tz == z),
                   lambda: pltpu.make_async_copy(own, jbuf.at[k, group, my_j], jrecv.at[group]).start(),
                   lambda: pltpu.make_async_remote_copy(
                       own, jbuf.at[k, group, my_j], jsend.at[g], jrecv.at[group],
                       device_id=device(xh * 2 + lax.rem(z, 2), y, tz, k), device_id_type=MESH).start())

    def plane_send(dx, dy):
        spot = BEHIND.index((4 - dy) % 4)
        pltpu.make_async_remote_copy(own, ibuf.at[spot * 4 + my_seg], isend, irecv.at[spot],
                                     device_id=device(lax.rem(x + dx, 4), lax.rem(y + dy, 4), z, xh), device_id_type=MESH).start()

    def left(ref, sem):
        return lambda: pltpu.make_async_copy(ref, ref, sem).wait()

    def ring_left(g):
        either(j_self & (group == g), left(ibuf.at[pl.ds(0, 3)], jsend.at[g]), left(ibuf.at[pl.ds(0, 4)], jsend.at[g]))

    ring_sends(0)
    for spot in range(4):
        dy = (4 - BEHIND[spot]) % 4
        for dx in (2, 1, 3):
            plane_send(dx, dy)
        if dy:
            plane_send(0, dy)
        else:
            either(i_self, lambda: pltpu.make_async_copy(own, ibuf.at[12 + my_seg], irecv.at[3]).start(), lambda: plane_send(0, 0))
    if not STAGED:
        ring_sends(1)

    if STAGED:
        ring_left(0)
        ring_sends(1)

    def here(buf, sem):
        pltpu.make_async_copy(buf, buf, sem).wait()

    for turn in range(2):
        g = group if turn == 0 else 1 - group
        here(jbuf.at[k, g], jrecv.at[g])
        pltpu.make_async_remote_copy(jbuf.at[k, g], jbuf.at[k, g], ksend.at[g], krecv.at[g],
                                     device_id=device(x, y, z, 1 - k), device_id_type=MESH).start()

    dot = functools.partial(jnp.dot, preferred_element_type=jnp.float32)
    scale = 1.0 / math.sqrt(half)
    my_o = y * 4 + x

    for part in range(16 // ROWS):
        here(ibuf.at[pl.ds(part * ROWS, ROWS)], irecv.at[part])

        @pl.loop(0, ROWS // 4)
        def _(n, part=part):
            for s in range(4):
                real = ibuf[ROWS * part + 4 * n + s, :, 0:half].astype(jnp.float32) * (gains[...] * scale)
                imag = ibuf[ROWS * part + 4 * n + s, :, half:].astype(jnp.float32) * (gains[...] * scale)
                ifull[n, s, :, 0:half] = real
                ifull[n, s, :, half:2 * half] = imag
                ifull[n, s, :, 2 * half:] = real + imag

        if part == 0:
            for g in range(2):
                here(jbuf.at[1 - k, g], krecv.at[g])
            for s in range(4):
                for g in range(2):
                    jfull[s, g] = jnp.concatenate([jbuf[s % 2, g, s // 2].astype(jnp.float32),
                                                   jbuf[s % 2, g, 2 + s // 2].astype(jnp.float32)], 0)

        def cross(t, u):
            offset = t * 256 + u * 128
            re = pl.ds(pl.multiple_of(offset, 128), 128)
            im = pl.ds(pl.multiple_of(half + offset, 128), 128)
            both = pl.ds(pl.multiple_of(2 * half + offset, 128), 128)
            cut = slice(u * 128, u * 128 + 128)
            jr = [[jfull[s, g, :, re] for g in range(2)] for s in range(4)]
            ji = [[jfull[s, g, :, im] for g in range(2)] for s in range(4)]
            jd = [[jr[s][g] - ji[s][g] for g in range(2)] for s in range(4)]
            for i in range(ROWS):
                ib = [ifull[i // 4, s, i % 4:i % 4 + 1, both] for s in range(4)]
                ir = [ifull[i // 4, s, i % 4:i % 4 + 1, re] for s in range(4)]
                ii = [ifull[i // 4, s, i % 4:i % 4 + 1, im] for s in range(4)]
                zr, zi = [], []
                for g in range(2):
                    rr = added([ir[s] * jr[s][g] for s in range(4)])
                    ss = added([ii[s] * ji[s][g] for s in range(4)])
                    bd = added([ib[s] * jd[s][g] for s in range(4)])
                    zr.append(rr + ss)
                    zi.append((rr - ss) - bd)
                for value, first in ((zr, 0), (zi, 16 * ROWS)):
                    rows = slice(first + i * 16, first + i * 16 + 16)
                    zh[t, rows, cut], zl[t, rows, cut] = split(jnp.concatenate(value, 0))

        @pl.loop(0, half // 256)
        def _(t, cross=cross):
            for u in range(2):
                cross(t, u)

        even = odd = 0.0
        edge = 16 * ROWS
        for t in range(half // 256):
            near = dot(zh[t], wh[...]) + dot(zl[t], wh[...]) + dot(zh[t], wl[...])
            c, d = steps[0, t:t + 1, :], steps[1, t:t + 1, :]
            even += c * near[0:edge, 0:128] - d * near[0:edge, 128:256]
            odd += d * near[edge:, 0:128] + c * near[edge:, 128:256]
        obuf[part, :, 0:128] = even + odd
        obuf[part, :, 128:256] = even - odd

        for n in range(ROWS):
            spot, r = part * ROWS // 4 + n // 4, n % 4
            block = obuf.at[part, pl.ds(n * 16, 16)]

            def give(block=block, spot=spot, r=r):
                pltpu.make_async_remote_copy(
                    block, rbuf.at[my_o], osend, orecv,
                    device_id=device(k * 2 + r // 2, lax.rem(y + BEHIND[spot], 4), z, r % 2), device_id_type=MESH).start()

            if BEHIND[spot]:
                give()
            else:
                either(i_self & (my_seg == r), lambda block=block: pltpu.make_async_copy(block, rbuf.at[my_o], orecv).start(), give)

    either(i_self, left(rbuf.at[pl.ds(0, 15)], osend), left(rbuf, osend))
    either(i_self, left(ibuf.at[pl.ds(0, 15)], isend), left(ibuf, isend))

    for g in range(1 if STAGED else 0, 2):
        ring_left(g)
    for g in range(2):
        pltpu.make_async_copy(jbuf.at[0, g], jbuf.at[0, g], ksend.at[g]).wait()

    here(rbuf, orecv)


def assemble(rbuf, out_ref, base, turned):
    for b in range(8):
        rows = []
        for m in range(4):
            rows += [rbuf[2 * b, 4 * m:4 * m + 4, :], rbuf[2 * b + 1, 4 * m:4 * m + 4, :]]
        base[b // 4, (b % 4) * 32:(b % 4) * 32 + 32, :] = jnp.concatenate(rows, 0)

    for h in range(2):
        cut = slice(h * 128, (h + 1) * 128)
        turned[...] = base[h].T
        out_ref[MAXLAG:, 0, cut] = turned[0:MAXLAG + 1]
        for lag in range(1, MAXLAG + 1):
            out_ref[MAXLAG - lag:MAXLAG - lag + 1, 0, cut] = turned[128 + lag:129 + lag]


def body(spectra, band_gain):
    half = band_gain.shape[0]
    f32, b16 = jnp.float32, jnp.bfloat16
    dma = pltpu.SemaphoreType.DMA
    blocks = pl.pallas_call(
        kernel,
        out_shape=jax.ShapeDtypeStruct((16, 16, 256), f32),
        in_specs=[pl.BlockSpec(memory_space=pltpu.HBM), pl.BlockSpec(memory_space=pltpu.HBM)],
        out_specs=pl.BlockSpec(memory_space=pl.ANY),
        scratch_shapes=[
            pltpu.VMEM((4, 2 * half), b16),
            pltpu.VMEM((1, half), f32),
            pltpu.VMEM((16, 4, 2 * half), b16),
            pltpu.VMEM((2, 2, 4, 4, 2 * half), b16),
            pltpu.VMEM((2, 4, 4, 3 * half), f32),
            pltpu.VMEM((4, 2, 8, 2 * half), f32),
            pltpu.VMEM((half // 256, 32 * ROWS, 256), b16),
            pltpu.VMEM((half // 256, 32 * ROWS, 256), b16),
            pltpu.VMEM((256, 256), b16),
            pltpu.VMEM((256, 256), b16),
            pltpu.VMEM((2, half // 256, 128), f32),
            pltpu.VMEM((16 // ROWS, 16 * ROWS, 256), f32),
            dma, dma, dma, dma((4,)), dma((2,)), dma((2,)), dma((2,)), dma((2,)), dma, dma,
        ],
        compiler_params=pltpu.CompilerParams(
            collective_id=0, has_side_effects=True, vmem_limit_bytes=58 * 2**20),
        name="correlate",
    )(spectra, band_gain.reshape(1, half))
    rows = pl.pallas_call(
        assemble,
        out_shape=jax.ShapeDtypeStruct((2 * MAXLAG + 1, 1, 256), f32),
        in_specs=[pl.BlockSpec(memory_space=pltpu.VMEM)],
        out_specs=pl.BlockSpec(memory_space=pltpu.VMEM),
        scratch_shapes=[pltpu.VMEM((2, 128, 256), f32), pltpu.VMEM((256, 128), f32)],
        name="assemble",
    )(blocks)
    return jnp.transpose(rows, (1, 0, 2))


def solution(mesh):
    return jax.shard_map(
        body,
        mesh=mesh,
        in_specs=(P("seg", "chan", None), P()),
        out_specs=P(("chan", "seg"), None, None),
        check_vma=False,
    )
```
